512 devices in a mesh: dp: 4 (over y_hi), ctx: 16 (over x, y_lo, core), tp: 8 (over z).
Axes of the slice: x: 4, y: 8 (y_hi: 4, y_lo: 2; y = y_hi * 2 + y_lo), z: 8, core: 2. Of those that a mesh axis runs over, the one named last changes fastest.
Arguments:
- queries: bfloat16 [16384, 64, 128], P(('dp', 'ctx'), 'tp'), parts along dimension 0, may hold values from -7 to 7, as said below
- keys: bfloat16 [16384, 8, 128], P(('dp', 'ctx'), 'tp'), parts along dimension 0, may hold values from -7 to 7, as said below
- values: bfloat16 [16384, 8, 128], P(('dp', 'ctx'), 'tp'), parts along dimension 0, may hold values from -6 to 6
- doc_lengths: int32 [48], P('dp'), parts along dimension 0, may hold values from 1 to 3072, 4096 in all
Outputs:
- attended: bfloat16 [16384, 64, 128], P(('dp', 'ctx'), 'tp'), parts along dimension 0
The draws below stay inside these ranges and needn't reach their ends.
There are 4 independent parts, one for each index of `dp`. The reference program is written for one: setup_inputs(seed, part) draws one part's arguments, and reference() takes and returns one part's arrays. A program takes and returns all parts, laid end to end along the dimension named above; each array names one. Nothing has to cross between parts.
Inputs may be any that keep to these rules, and one draw needn't show every extreme that they name: `queries`: query entries lie within the bounds. `keys`: key entries lie within the bounds.
All inputs are finite; a program needn't handle non-finite values.
Results may differ from the reference program's by a relative error of at most 0.004.
Values may be sent and summed in bfloat16 or wider, within the bound.
No kernel may reach another device: no remote copies, remote signals or barrier semaphores. Data moves between devices by JAX's collectives and lax.ppermute only.
A program may use at most 64 MiB of HBM per device.

```python
import math
import jax
import jax.numpy as jnp
import numpy as np
from jax import lax

H = 64
KVH = 8
HD = 128
NDOC = 12
SEQ = 4096


def draw_queries(key, part):
    key = jax.random.fold_in(key, 11)
    result = jnp.clip(jax.random.normal(key, (SEQ, H, HD)), -6.0, 6.0)
    return result.astype(jnp.bfloat16)


def draw_keys(key, part):
    key = jax.random.fold_in(key, 12)
    result = jnp.clip(jax.random.normal(key, (SEQ, KVH, HD)), -6.0, 6.0)
    return result.astype(jnp.bfloat16)


def steps_of(stream_key, dims, pieces, low, high):
    level = 1.0
    for position, blocks in pieces:
        heights = jax.random.uniform(jax.random.fold_in(jax.random.fold_in(stream_key, 6), position), (blocks,), jnp.float32, low / len(pieces), high / len(pieces))
        level = level * jnp.repeat(jnp.exp(heights), dims[position] // blocks).reshape((-1,) + (1,) * (len(dims) - 1 - position))
    return level


def profile(count, total, most, slope):
    weights = [(1 << 20) // math.isqrt(standing ** slope) + 1 for standing in range(2, count + 1)]
    rest, counts = total - most - (count - 1), [1] * (count - 1)
    while rest > 0:
        free = [i for i in range(count - 1) if counts[i] < most]
        pool, budget = sum([weights[i] for i in free]), rest
        for i in free:
            more = min(most - counts[i], max(1, budget * weights[i] // pool), rest)
            counts[i] = counts[i] + more
            rest = rest - more
    return np.array([most] + counts)


def uneven_parts(stream_key, amount, total, limit, skew):
    if amount == 2:
        one = jax.random.randint(stream_key, (), max(1, total - limit), min(limit, total - 1) + 1)
        return jnp.stack([one, total - one])
    lengths = jnp.asarray(profile(amount, total, limit, skew), jnp.int32)
    pairs = (amount - 1) // 2
    giver, sink = lengths[1:1 + 2 * pairs:2], lengths[2:2 + 2 * pairs:2]
    room = jnp.minimum(giver - 1, limit - sink)
    shifted = jax.random.randint(jax.random.fold_in(stream_key, 1), (pairs,), 0, 1 << 20) % (room + 1)
    lengths = lengths.at[1:1 + 2 * pairs:2].set(giver - shifted).at[2:2 + 2 * pairs:2].set(sink + shifted)
    return lengths[jax.random.permutation(jax.random.fold_in(stream_key, 2), amount)]


def scatter_about(rng, dims, spread, bound, pieces=(), kind=jnp.bfloat16):
    array = spread * jax.random.normal(rng, dims, jnp.float32)
    if pieces:
        array = array * steps_of(rng, dims, pieces, -0.22, 0.18)
    return jnp.clip(array, -bound, bound).astype(kind)


def setup_inputs(seed: int = 0, part: int = 0) -> dict:
    key_of = jax.random.split(jax.random.key(seed), 5)
    part_keys = jax.random.split(jax.random.fold_in(key_of[4], part), 5)
    queries = draw_queries(jax.random.fold_in(jax.random.fold_in(key_of[4], part), 71), part)
    keys = draw_keys(jax.random.fold_in(jax.random.fold_in(key_of[4], part), 71), part)
    values = scatter_about(part_keys[2], (SEQ, KVH, HD), 1.0, 6.0, ((0, 16), (1, 8)))
    doc_lengths = uneven_parts(part_keys[3], NDOC, SEQ, SEQ * 3 // 4, 2).astype(jnp.int32)
    return dict(queries=queries, keys=keys, values=values, doc_lengths=doc_lengths)


def reference(queries, keys, values, doc_lengths):
    positions = jnp.arange(SEQ, dtype=jnp.int32)
    doc_ends = jnp.cumsum(doc_lengths).astype(jnp.int32)
    doc_starts = (doc_ends - doc_lengths).astype(jnp.int32)
    query_start = jnp.max(jnp.where(doc_starts[None, :] <= positions[:, None], doc_starts[None, :], 0), axis=1)
    visible_mask = (positions[None, :] <= positions[:, None]) & (positions[None, :] >= query_start[:, None])
    group_size = H // KVH
    score_scale = HD ** -0.5

    def one_head(head_index):
        query_head = lax.dynamic_index_in_dim(queries, head_index, 1, keepdims=False)
        kv_index = head_index // group_size
        key_head = lax.dynamic_index_in_dim(keys, kv_index, 1, keepdims=False)
        value_head = lax.dynamic_index_in_dim(values, kv_index, 1, keepdims=False)
        tile_scores = jnp.dot(query_head, key_head.T, preferred_element_type=jnp.float32) * score_scale
        tile_scores = jnp.where(visible_mask, tile_scores, -jnp.inf)
        row_best = jnp.max(tile_scores, axis=1, keepdims=True)
        exponent = jnp.exp(tile_scores - row_best)
        row_total = jnp.sum(exponent, axis=1, keepdims=True)
        mixed = jnp.dot(exponent.astype(jnp.bfloat16), value_head, preferred_element_type=jnp.float32) / row_total
        return mixed.astype(jnp.bfloat16)

    heads_out = lax.map(one_head, jnp.arange(H, dtype=jnp.int32))
    return jnp.transpose(heads_out, (1, 0, 2))
```

```python
import functools

import jax
import jax.numpy as jnp
from jax import lax
from jax.experimental import pallas as pl
from jax.experimental.pallas import tpu as pltpu
from jax.sharding import PartitionSpec as P

HEAD = 128
CHUNK = 256
LOG2_SCALE = HEAD**-0.5 * 1.4426950408889634
LOWEST = -1e30


def flash(lengths, q, mine, theirs, out, best, total, acc, starts):
    rows = q.shape[0]
    group = rows // CHUNK
    position = lax.axis_index("ctx")
    core = lax.rem(position, 2)
    tile_id = position // 2
    first = position * CHUNK
    last = first + CHUNK - 1
    token = first + lax.broadcasted_iota(jnp.int32, (CHUNK, HEAD), 0)
    begin = jnp.int32(0)
    first_start, last_start = jnp.int32(0), jnp.int32(0)
    token_start = jnp.zeros((CHUNK, HEAD), jnp.int32)
    for doc in range(lengths.shape[0]):
        token_start = jnp.where(token >= begin, begin, token_start)
        first_start = jnp.where(first >= begin, begin, first_start)
        last_start = jnp.where(last >= begin, begin, last_start)
        begin = begin + lengths[doc]
    for head in range(group):
        starts[pl.ds(head, CHUNK, stride=group), :] = token_start
    best[...] = jnp.full(best.shape, LOWEST, jnp.float32)
    total[...] = jnp.zeros(total.shape, jnp.float32)
    acc[...] = jnp.zeros(acc.shape, jnp.float32)

    def fold(tile, masked):
        halves = ((mine, 2 * tile + core), (theirs, 2 * tile + 1 - core))
        scores = [
            lax.dot_general(
                q[...], ref[tile, 0], (((1,), (1,)), ((), ())), preferred_element_type=jnp.float32
            )
            for ref, _ in halves
        ]
        blocks = []
        for part, (_, chunk) in zip(scores, halves):
            for j in range(0, CHUNK, HEAD):
                block = part[:, j : j + HEAD]
                if masked:
                    key = chunk * CHUNK + j + lax.broadcasted_iota(jnp.int32, block.shape, 1)
                    row = first + lax.broadcasted_iota(jnp.int32, block.shape, 0) // group
                    block = jnp.where((key >= starts[...]) & (key <= row), block, LOWEST)
                blocks.append(block)
        peak = functools.reduce(jnp.maximum, blocks)
        old = best[...]
        new = jnp.maximum(old, jnp.max(peak, axis=1, keepdims=True))
        shrink = jnp.exp2((old - new) * LOG2_SCALE)
        base = new * LOG2_SCALE
        weights = [jnp.exp2(block * LOG2_SCALE - base) for block in blocks]
        best[...] = new
        total[...] = total[...] * shrink + sum(weights)
        low = [w.astype(jnp.bfloat16) for w in weights]
        half = len(low) // 2
        added = jnp.dot(
            jnp.concatenate(low[:half], 1), mine[tile, 1], preferred_element_type=jnp.float32
        ) + jnp.dot(
            jnp.concatenate(low[half:], 1), theirs[tile, 1], preferred_element_type=jnp.float32
        )
        acc[...] = acc[...] * shrink + added

    fold(tile_id, True)

    def step(tile, carry):
        clear = tile * 2 * CHUNK >= last_start

        @pl.when(clear)
        def _():
            fold(tile, False)

        @pl.when(jnp.logical_not(clear))
        def _():
            fold(tile, True)

        return carry

    lax.fori_loop(first_start // (2 * CHUNK), tile_id, step, 0)
    out[...] = (acc[...] / jnp.sum(total[...], axis=1, keepdims=True)).astype(out.dtype)


def per_device(queries, keys, values, doc_lengths):
    tokens, heads, _ = queries.shape
    rows = tokens * heads
    q = queries.reshape(rows, HEAD)
    kv = jnp.stack([keys[:, 0], values[:, 0]])
    spread = jnp.broadcast_to(kv[None], (8,) + kv.shape)
    groups = [[2 * i + core for i in range(8)] for core in range(2)]
    mine = lax.all_to_all(spread, "ctx", 0, 0, axis_index_groups=groups)
    theirs = lax.ppermute(mine, "ctx", [(i, i ^ 1) for i in range(16)])
    vmem = pl.BlockSpec(memory_space=pltpu.VMEM)
    out = pl.pallas_call(
        flash,
        out_shape=jax.ShapeDtypeStruct((rows, HEAD), jnp.bfloat16),
        in_specs=[pl.BlockSpec(memory_space=pltpu.SMEM), vmem, vmem, vmem],
        out_specs=vmem,
        scratch_shapes=[pltpu.VMEM((rows, HEAD), jnp.float32)] * 3
        + [pltpu.VMEM((rows, HEAD), jnp.int32)],
        compiler_params=pltpu.CompilerParams(vmem_limit_bytes=48 * 2**20),
    )(doc_lengths, q, mine, theirs)
    return out.reshape(queries.shape)


def solution(mesh):
    placed = (
        P(("dp", "ctx"), "tp", None),
        P(("dp", "ctx"), "tp", None),
        P(("dp", "ctx"), "tp", None),
        P("dp"),
    )
    return jax.shard_map(
        per_device,
        mesh=mesh,
        in_specs=placed,
        out_specs=P(("dp", "ctx"), "tp", None),
        check_vma=False,
    )
```

```python
import functools

import jax
import jax.numpy as jnp
from jax import lax
from jax.experimental import pallas as pl
from jax.experimental.pallas import tpu as pltpu
from jax.sharding import PartitionSpec as P

HEAD = 128
CHUNK = 256
BLOCK = 512
LOG2_SCALE = HEAD**-0.5 * 1.4426950408889634
LOWEST = -1e30
HIDDEN = 1e30
SLACK = 40.0 / LOG2_SCALE
VMEM_LIMIT = 20 * 2**20


def place(lengths):
    position = lax.axis_index("ctx")
    first = position * CHUNK
    begin = jnp.int32(0)
    first_start = jnp.int32(0)
    begins = []
    for doc in range(lengths.shape[0]):
        begins.append(begin)
        first_start = jnp.where(first >= begin, begin, first_start)
        begin = begin + lengths[doc]
    return position, first, first_start, begins


def scores(q, key):
    return lax.dot_general(q, key, (((1,), (1,)), ((), ())), preferred_element_type=jnp.float32)


def split(block):
    return [block[:, j : j + HEAD] for j in range(0, CHUNK, HEAD)]


def hide(block, chunk, first, row0, group, starts):
    done = []
    for j, part in enumerate(split(block)):
        key = chunk * CHUNK + j * HEAD + lax.broadcasted_iota(jnp.int32, part.shape, 1)
        row = first + (row0 + lax.broadcasted_iota(jnp.int32, part.shape, 0)) // group
        done.append(jnp.where((key >= starts) & (key <= row), part, LOWEST))
    return jnp.concatenate(done, 1)


def local_kernel(lengths, q, own, partner, best, total, acc, starts):
    rows = q.shape[0]
    group = rows // CHUNK
    position, first, first_start, begins = place(lengths)
    core = lax.rem(position, 2)
    token = first + lax.broadcasted_iota(jnp.int32, (CHUNK, HEAD), 0)
    token_start = jnp.zeros((CHUNK, HEAD), jnp.int32)
    for begin in begins:
        token_start = jnp.where(token >= begin, begin, token_start)
    for head in range(group):
        starts[pl.ds(head, CHUNK, stride=group), :] = token_start
    best[...] = jnp.full(best.shape, LOWEST, jnp.float32)
    total[...] = jnp.zeros(total.shape, jnp.float32)
    acc[...] = jnp.zeros(acc.shape, jnp.float32)

    def fold(ref, chunk):
        def block(i, carry):
            rs = pl.ds(pl.multiple_of(i * BLOCK, BLOCK), BLOCK)
            s = hide(scores(q[rs, :], ref[0]), chunk, first, i * BLOCK, group, starts[rs, :])
            old = best[rs, :]
            new = jnp.maximum(old, jnp.max(s, axis=1, keepdims=True))
            shrink = jnp.exp2((old - new) * LOG2_SCALE)
            base = new * LOG2_SCALE
            weights = [jnp.exp2(part * LOG2_SCALE - base) for part in split(s)]
            best[rs, :] = new
            total[rs, :] = total[rs, :] * shrink + sum(weights)
            low = jnp.concatenate([w.astype(jnp.bfloat16) for w in weights], 1)
            acc[rs, :] = acc[rs, :] * shrink + jnp.dot(
                low, ref[1], preferred_element_type=jnp.float32
            )
            return carry

        lax.fori_loop(0, rows // BLOCK, block, 0)

    @pl.when(core == 1)
    def _():
        fold(partner, position - 1)

    fold(own, position)
    best[...] = jnp.where(starts[...] == first_start, best[...], HIDDEN)


def fold_chunks(lengths, q, kv, best, total, acc, here, there, mine):
    rows = q.shape[0]
    position, _, first_start, _ = place(lengths)
    core = lax.rem(position, 2)
    core = core if mine else 1 - core
    lo = (first_start // CHUNK - core + 1) // 2
    hi = position // 2

    def excess_of(s, rs):
        excess = functools.reduce(jnp.maximum, split(s)) - best[rs, :]
        return jnp.max(excess.reshape(BLOCK // 8, 8, HEAD), axis=0)

    def flag_of(over):
        return (jnp.max(over) > SLACK).astype(jnp.int32)

    def first_scores():
        key = (2 * lo + core) * CHUNK + lax.broadcasted_iota(jnp.int32, (1, CHUNK), 1)
        seen = key >= first_start
        over = None
        for r in range(0, rows, BLOCK):
            rs = slice(r, r + BLOCK)
            s = jnp.where(seen, scores(q[rs, :], kv[lo, 0]), LOWEST)
            here[rs, :] = s
            excess = excess_of(s, rs)
            over = excess if over is None else jnp.maximum(over, excess)
        return flag_of(over)

    def mend(now):
        def block(i, carry):
            rs = pl.ds(pl.multiple_of(i * BLOCK, BLOCK), BLOCK)
            old = best[rs, :]
            new = jnp.maximum(old, jnp.max(now[rs, :], axis=1, keepdims=True))
            shrink = jnp.exp2((old - new) * LOG2_SCALE)
            best[rs, :] = new
            total[rs, :] = total[rs, :] * shrink
            acc[rs, :] = acc[rs, :] * shrink
            return carry

        lax.fori_loop(0, rows // BLOCK, block, 0)

    def step(tile, now, later, stale):
        @pl.when(stale > 0)
        def _():
            mend(now)

        ahead = jnp.minimum(tile + 1, hi - 1)
        over = None
        for r in range(0, rows, BLOCK):
            rs = slice(r, r + BLOCK)
            s = scores(q[rs, :], kv[ahead, 0])
            later[rs, :] = s
            excess = excess_of(s, rs)
            over = excess if over is None else jnp.maximum(over, excess)
            base = best[rs, :] * LOG2_SCALE
            weights = [jnp.exp2(part * LOG2_SCALE - base) for part in split(now[rs, :])]
            total[rs, :] += sum(weights)
            low = jnp.concatenate([w.astype(jnp.bfloat16) for w in weights], 1)
            acc[rs, :] += jnp.dot(low, kv[tile, 1], preferred_element_type=jnp.float32)
        return flag_of(over)

    @pl.when(lo < hi)
    def _():
        stale = first_scores()

        def pair(i, stale):
            tile = lo + 2 * i
            stale = step(tile, here, there, stale)
            return lax.cond(
                tile + 1 < hi,
                lambda flag: step(tile + 1, there, here, flag),
                lambda flag: flag,
                stale,
            )

        lax.fori_loop(0, (hi - lo + 1) // 2, pair, stale)


def middle_kernel(
    lengths, q, kv, best_in, total_in, acc_in, best, total, acc, here, there
):
    best[...], total[...], acc[...] = best_in[...], total_in[...], acc_in[...]
    fold_chunks(lengths, q, kv, best, total, acc, here, there, True)


def last_kernel(
    lengths, q, kv, best_in, total_in, acc_in, out, best, total, acc, here, there
):
    best[...], total[...], acc[...] = best_in[...], total_in[...], acc_in[...]
    fold_chunks(lengths, q, kv, best, total, acc, here, there, False)
    for r in range(0, out.shape[0], BLOCK):
        rs = slice(r, r + BLOCK)
        out[rs, :] = (acc[rs, :] / jnp.sum(total[rs, :], axis=1, keepdims=True)).astype(out.dtype)


def per_device(queries, keys, values, doc_lengths):
    tokens, heads, _ = queries.shape
    rows = tokens * heads
    q = queries.reshape(rows, HEAD)
    spread = jnp.broadcast_to(
        jnp.stack([keys[:, 0], values[:, 0]])[None], (8, 2, tokens, HEAD)
    )
    near_keys, near_values = lax.optimization_barrier((keys, values))
    kv = jnp.stack([near_keys[:, 0], near_values[:, 0]])
    groups = [[2 * i + core for i in range(8)] for core in range(2)]
    swap = [(i, i ^ 1) for i in range(16)]
    mine = lax.all_to_all(spread, "ctx", 0, 0, axis_index_groups=groups)
    partner = lax.ppermute(kv, "ctx", swap)

    smem = pl.BlockSpec(memory_space=pltpu.SMEM)
    vmem = pl.BlockSpec(memory_space=pltpu.VMEM)
    params = pltpu.CompilerParams(vmem_limit_bytes=VMEM_LIMIT)
    wide = jax.ShapeDtypeStruct((rows, HEAD), jnp.float32)
    holds = [pltpu.VMEM((rows, CHUNK), jnp.float32)] * 2
    best, total, acc = pl.pallas_call(
        local_kernel,
        out_shape=(wide, wide, wide),
        in_specs=[smem, vmem, vmem, vmem],
        out_specs=(vmem, vmem, vmem),
        scratch_shapes=[pltpu.VMEM((rows, HEAD), jnp.int32)],
        compiler_params=params,
        cost_estimate=pl.CostEstimate(
            flops=6 * rows * CHUNK * HEAD * 4, bytes_accessed=2**24, transcendentals=0
        ),
    )(doc_lengths, q, kv, partner)
    mine, best, total, acc = lax.optimization_barrier((mine, best, total, acc))
    theirs = lax.ppermute(mine, "ctx", swap)
    best, total, acc = pl.pallas_call(
        middle_kernel,
        out_shape=(wide, wide, wide),
        in_specs=[smem] + [vmem] * 5,
        out_specs=(vmem, vmem, vmem),
        scratch_shapes=holds,
        compiler_params=params,
        cost_estimate=pl.CostEstimate(
            flops=14 * rows * CHUNK * HEAD * 4, bytes_accessed=2**24, transcendentals=0
        ),
    )(doc_lengths, q, mine, best, total, acc)
    out = pl.pallas_call(
        last_kernel,
        out_shape=jax.ShapeDtypeStruct((rows, HEAD), jnp.bfloat16),
        in_specs=[smem] + [vmem] * 5,
        out_specs=vmem,
        scratch_shapes=[pltpu.VMEM((rows, HEAD), jnp.float32)] * 3 + holds,
        compiler_params=params,
        cost_estimate=pl.CostEstimate(
            flops=14 * rows * CHUNK * HEAD * 4, bytes_accessed=2**24, transcendentals=0
        ),
    )(doc_lengths, q, theirs, best, total, acc)
    return out.reshape(queries.shape)


def solution(mesh):
    placed = (
        P(("dp", "ctx"), "tp", None),
        P(("dp", "ctx"), "tp", None),
        P(("dp", "ctx"), "tp", None),
        P("dp"),
    )
    return jax.shard_map(
        per_device,
        mesh=mesh,
        in_specs=placed,
        out_specs=P(("dp", "ctx"), "tp", None),
        check_vma=False,
    )
```

```python
import functools

import jax
import jax.numpy as jnp
from jax import lax
from jax.experimental import pallas as pl
from jax.experimental.pallas import tpu as pltpu
from jax.sharding import PartitionSpec as P

HEAD = 128
CHUNK = 256
BLOCK = 512
LOG2_SCALE = HEAD**-0.5 * 1.4426950408889634
LOWEST = -1e30
HIDDEN = 1e30
SLACK = 40.0 / LOG2_SCALE
VMEM_LIMIT = 20 * 2**20


def place(lengths):
    position = lax.axis_index("ctx")
    first = position * CHUNK
    begin = jnp.int32(0)
    first_start = jnp.int32(0)
    begins = []
    for doc in range(lengths.shape[0]):
        begins.append(begin)
        first_start = jnp.where(first >= begin, begin, first_start)
        begin = begin + lengths[doc]
    return position, first, first_start, begins


def scores(q, key):
    return lax.dot_general(q, key, (((1,), (1,)), ((), ())), preferred_element_type=jnp.float32)


def split(block):
    return [block[:, j : j + HEAD] for j in range(0, CHUNK, HEAD)]


def hide(block, chunk, first, row0, group, starts):
    done = []
    for j, part in enumerate(split(block)):
        key = chunk * CHUNK + j * HEAD + lax.broadcasted_iota(jnp.int32, part.shape, 1)
        row = first + (row0 + lax.broadcasted_iota(jnp.int32, part.shape, 0)) // group
        done.append(jnp.where((key >= starts) & (key <= row), part, LOWEST))
    return jnp.concatenate(done, 1)


def local_kernel(lengths, q, own, partner, best, total, acc, starts):
    rows = q.shape[0]
    group = rows // CHUNK
    position, first, first_start, begins = place(lengths)
    core = lax.rem(position, 2)
    token = first + lax.broadcasted_iota(jnp.int32, (CHUNK, HEAD), 0)
    token_start = jnp.zeros((CHUNK, HEAD), jnp.int32)
    for begin in begins:
        token_start = jnp.where(token >= begin, begin, token_start)
    for head in range(group):
        starts[pl.ds(head, CHUNK, stride=group), :] = token_start
    best[...] = jnp.full(best.shape, LOWEST, jnp.float32)
    total[...] = jnp.zeros(total.shape, jnp.float32)
    acc[...] = jnp.zeros(acc.shape, jnp.float32)

    def fold(ref, chunk):
        def block(i, carry):
            rs = pl.ds(pl.multiple_of(i * BLOCK, BLOCK), BLOCK)
            s = hide(scores(q[rs, :], ref[0]), chunk, first, i * BLOCK, group, starts[rs, :])
            old = best[rs, :]
            new = jnp.maximum(old, jnp.max(s, axis=1, keepdims=True))
            shrink = jnp.exp2((old - new) * LOG2_SCALE)
            base = new * LOG2_SCALE
            weights = [jnp.exp2(part * LOG2_SCALE - base) for part in split(s)]
            best[rs, :] = new
            total[rs, :] = total[rs, :] * shrink + sum(weights)
            low = jnp.concatenate([w.astype(jnp.bfloat16) for w in weights], 1)
            acc[rs, :] = acc[rs, :] * shrink + jnp.dot(
                low, ref[1], preferred_element_type=jnp.float32
            )
            return carry

        lax.fori_loop(0, rows // BLOCK, block, 0)

    @pl.when(core == 1)
    def _():
        fold(partner, position - 1)

    fold(own, position)
    best[...] = jnp.where(starts[...] == first_start, best[...], HIDDEN)


def fold_chunks(lengths, q, kv, best, total, acc, here, there, mine):
    rows = q.shape[0]
    position, _, first_start, _ = place(lengths)
    core = lax.rem(position, 2)
    core = core if mine else 1 - core
    lo = (first_start // CHUNK - core + 1) // 2
    hi = position // 2

    def excess_of(s, rs):
        excess = functools.reduce(jnp.maximum, split(s)) - best[rs, :]
        return jnp.max(excess.reshape(BLOCK // 8, 8, HEAD), axis=0)

    def flag_of(over):
        return (jnp.max(over) > SLACK).astype(jnp.int32)

    def first_scores():
        key = (2 * lo + core) * CHUNK + lax.broadcasted_iota(jnp.int32, (1, CHUNK), 1)
        seen = key >= first_start
        over = None
        for r in range(0, rows, BLOCK):
            rs = slice(r, r + BLOCK)
            s = jnp.where(seen, scores(q[rs, :], kv[lo, 0]), LOWEST)
            here[rs, :] = s
            excess = excess_of(s, rs)
            over = excess if over is None else jnp.maximum(over, excess)
        return flag_of(over)

    def mend(now):
        def block(i, carry):
            rs = pl.ds(pl.multiple_of(i * BLOCK, BLOCK), BLOCK)
            old = best[rs, :]
            new = jnp.maximum(old, jnp.max(now[rs, :], axis=1, keepdims=True))
            shrink = jnp.exp2((old - new) * LOG2_SCALE)
            best[rs, :] = new
            total[rs, :] = total[rs, :] * shrink
            acc[rs, :] = acc[rs, :] * shrink
            return carry

        lax.fori_loop(0, rows // BLOCK, block, 0)

    def step(tile, now, later, stale):
        @pl.when(stale > 0)
        def _():
            mend(now)

        ahead = jnp.minimum(tile + 1, hi - 1)
        over = None
        for r in range(0, rows, BLOCK):
            rs = slice(r, r + BLOCK)
            s = scores(q[rs, :], kv[ahead, 0])
            later[rs, :] = s
            excess = excess_of(s, rs)
            over = excess if over is None else jnp.maximum(over, excess)
            base = best[rs, :] * LOG2_SCALE
            weights = [jnp.exp2(part * LOG2_SCALE - base) for part in split(now[rs, :])]
            total[rs, :] += sum(weights)
            low = jnp.concatenate([w.astype(jnp.bfloat16) for w in weights], 1)
            acc[rs, :] += jnp.dot(low, kv[tile, 1], preferred_element_type=jnp.float32)
        return flag_of(over)

    @pl.when(lo < hi)
    def _():
        stale = first_scores()

        def pair(i, stale):
            tile = lo + 2 * i
            stale = step(tile, here, there, stale)
            return lax.cond(
                tile + 1 < hi,
                lambda flag: step(tile + 1, there, here, flag),
                lambda flag: flag,
                stale,
            )

        lax.fori_loop(0, (hi - lo + 1) // 2, pair, stale)


def middle_kernel(lengths, q, kv, near_best, best, total, acc, here, there):
    best[...] = near_best[...]
    total[...] = jnp.zeros(total.shape, jnp.float32)
    acc[...] = jnp.zeros(acc.shape, jnp.float32)
    fold_chunks(lengths, q, kv, best, total, acc, here, there, True)


def last_kernel(
    lengths,
    q,
    kv,
    near_best,
    near_total,
    near_acc,
    best_in,
    total_in,
    acc_in,
    out,
    best,
    total,
    acc,
    here,
    there,
):
    for r in range(0, out.shape[0], BLOCK):
        rs = slice(r, r + BLOCK)
        shrink = jnp.exp2((near_best[rs, :] - best_in[rs, :]) * LOG2_SCALE)
        best[rs, :] = best_in[rs, :]
        total[rs, :] = total_in[rs, :] + near_total[rs, :] * shrink
        acc[rs, :] = acc_in[rs, :] + near_acc[rs, :] * shrink
    fold_chunks(lengths, q, kv, best, total, acc, here, there, False)
    for r in range(0, out.shape[0], BLOCK):
        rs = slice(r, r + BLOCK)
        out[rs, :] = (acc[rs, :] / jnp.sum(total[rs, :], axis=1, keepdims=True)).astype(out.dtype)


def per_device(queries, keys, values, doc_lengths):
    tokens, heads, _ = queries.shape
    rows = tokens * heads
    q = queries.reshape(rows, HEAD)
    spread = jnp.broadcast_to(
        jnp.stack([keys[:, 0], values[:, 0]])[None], (8, 2, tokens, HEAD)
    )
    near_keys, near_values = lax.optimization_barrier((keys, values))
    kv = jnp.stack([near_keys[:, 0], near_values[:, 0]])
    groups = [[2 * i + core for i in range(8)] for core in range(2)]
    swap = [(i, i ^ 1) for i in range(16)]
    mine = lax.all_to_all(spread, "ctx", 0, 0, axis_index_groups=groups)
    partner = lax.ppermute(kv, "ctx", swap)

    smem = pl.BlockSpec(memory_space=pltpu.SMEM)
    vmem = pl.BlockSpec(memory_space=pltpu.VMEM)
    params = pltpu.CompilerParams(vmem_limit_bytes=VMEM_LIMIT)
    wide = jax.ShapeDtypeStruct((rows, HEAD), jnp.float32)
    holds = [pltpu.VMEM((rows, CHUNK), jnp.float32)] * 2
    near = pl.pallas_call(
        local_kernel,
        out_shape=(wide, wide, wide),
        in_specs=[smem, vmem, vmem, vmem],
        out_specs=(vmem, vmem, vmem),
        scratch_shapes=[pltpu.VMEM((rows, HEAD), jnp.int32)],
        compiler_params=params,
        cost_estimate=pl.CostEstimate(
            flops=6 * rows * CHUNK * HEAD * 4, bytes_accessed=2**24, transcendentals=0
        ),
    )(doc_lengths, q, kv, partner)
    mine, near_best = lax.optimization_barrier((mine, near[0]))
    theirs = lax.ppermute(mine, "ctx", swap)
    far = pl.pallas_call(
        middle_kernel,
        out_shape=(wide, wide, wide),
        in_specs=[smem] + [vmem] * 3,
        out_specs=(vmem, vmem, vmem),
        scratch_shapes=holds,
        compiler_params=params,
        cost_estimate=pl.CostEstimate(
            flops=14 * rows * CHUNK * HEAD * 4, bytes_accessed=2**24, transcendentals=0
        ),
    )(doc_lengths, q, mine, near_best)
    out = pl.pallas_call(
        last_kernel,
        out_shape=jax.ShapeDtypeStruct((rows, HEAD), jnp.bfloat16),
        in_specs=[smem] + [vmem] * 8,
        out_specs=vmem,
        scratch_shapes=[pltpu.VMEM((rows, HEAD), jnp.float32)] * 3 + holds,
        compiler_params=params,
        cost_estimate=pl.CostEstimate(
            flops=14 * rows * CHUNK * HEAD * 4, bytes_accessed=2**24, transcendentals=0
        ),
    )(doc_lengths, q, theirs, *near, *far)
    return out.reshape(queries.shape)


def solution(mesh):
    placed = (
        P(("dp", "ctx"), "tp", None),
        P(("dp", "ctx"), "tp", None),
        P(("dp", "ctx"), "tp", None),
        P("dp"),
    )
    return jax.shard_map(
        per_device,
        mesh=mesh,
        in_specs=placed,
        out_specs=P(("dp", "ctx"), "tp", None),
        check_vma=False,
    )
```

```python
import functools

import jax
import jax.numpy as jnp
from jax import lax
from jax.experimental import pallas as pl
from jax.experimental.pallas import tpu as pltpu
from jax.sharding import PartitionSpec as P

HEAD = 128
CHUNK = 256
BLOCK = 512
LOG2_SCALE = HEAD**-0.5 * 1.4426950408889634
LOWEST = -1e30
HIDDEN = 1e30
SLACK = 40.0 / LOG2_SCALE
REACH = 100.0 / LOG2_SCALE
VMEM_LIMIT = 20 * 2**20


def place(lengths):
    position = lax.axis_index("ctx")
    first = position * CHUNK
    begin = jnp.int32(0)
    first_start = jnp.int32(0)
    begins = []
    for doc in range(lengths.shape[0]):
        begins.append(begin)
        first_start = jnp.where(first >= begin, begin, first_start)
        begin = begin + lengths[doc]
    return position, first, first_start, begins


def scores(q, key):
    return lax.dot_general(q, key, (((1,), (1,)), ((), ())), preferred_element_type=jnp.float32)


def split(block):
    return [block[:, j : j + HEAD] for j in range(0, CHUNK, HEAD)]


def hide(block, chunk, first, row0, group, starts):
    done = []
    for j, part in enumerate(split(block)):
        key = chunk * CHUNK + j * HEAD + lax.broadcasted_iota(jnp.int32, part.shape, 1)
        row = first + (row0 + lax.broadcasted_iota(jnp.int32, part.shape, 0)) // group
        done.append(jnp.where((key >= starts) & (key <= row), part, LOWEST))
    return jnp.concatenate(done, 1)


def local_kernel(lengths, q, own, partner, best, total, acc, reach, starts):
    rows = q.shape[0]
    group = rows // CHUNK
    position, first, first_start, begins = place(lengths)
    core = lax.rem(position, 2)
    token = first + lax.broadcasted_iota(jnp.int32, (CHUNK, HEAD), 0)
    token_start = jnp.zeros((CHUNK, HEAD), jnp.int32)
    for begin in begins:
        token_start = jnp.where(token >= begin, begin, token_start)
    for head in range(group):
        starts[pl.ds(head, CHUNK, stride=group), :] = token_start
    best[...] = jnp.full(best.shape, LOWEST, jnp.float32)
    total[...] = jnp.zeros(total.shape, jnp.float32)
    acc[...] = jnp.zeros(acc.shape, jnp.float32)

    def fold(ref, chunk):
        def block(i, carry):
            rs = pl.ds(pl.multiple_of(i * BLOCK, BLOCK), BLOCK)
            s = hide(scores(q[rs, :], ref[0]), chunk, first, i * BLOCK, group, starts[rs, :])
            old = best[rs, :]
            new = jnp.maximum(old, jnp.max(s, axis=1, keepdims=True))
            shrink = jnp.exp2((old - new) * LOG2_SCALE)
            base = new * LOG2_SCALE
            weights = [jnp.exp2(part * LOG2_SCALE - base) for part in split(s)]
            best[rs, :] = new
            total[rs, :] = total[rs, :] * shrink + sum(weights)
            low = jnp.concatenate([w.astype(jnp.bfloat16) for w in weights], 1)
            acc[rs, :] = acc[rs, :] * shrink + jnp.dot(
                low, ref[1], preferred_element_type=jnp.float32
            )
            return carry

        lax.fori_loop(0, rows // BLOCK, block, 0)

    @pl.when(core == 1)
    def _():
        fold(partner, position - 1)

    fold(own, position)
    longest = jnp.zeros((8, HEAD), jnp.float32)
    least = jnp.full((8, HEAD), HIDDEN, jnp.float32)
    for r in range(0, rows, BLOCK):
        rs = slice(r, r + BLOCK)
        kept = jnp.where(starts[rs, :] == first_start, best[rs, :], HIDDEN)
        best[rs, :] = kept
        least = jnp.minimum(least, jnp.min(kept.reshape(BLOCK // 8, 8, HEAD), axis=0))
        squares = jnp.square(q[rs, :].astype(jnp.float32))
        norms = jnp.broadcast_to(jnp.sum(squares, axis=1, keepdims=True), squares.shape)
        longest = jnp.maximum(longest, jnp.max(norms.reshape(BLOCK // 8, 8, HEAD), axis=0))
    reach[0] = jnp.broadcast_to(jnp.max(longest, axis=0, keepdims=True), (8, HEAD))
    reach[1] = jnp.broadcast_to(jnp.min(least, axis=0, keepdims=True), (8, HEAD))


def fold_chunks(lengths, q, kv, reach, best, total, acc, here, there, mine):
    rows = q.shape[0]
    position, _, first_start, _ = place(lengths)
    core = lax.rem(position, 2)
    core = core if mine else 1 - core
    lo = (first_start // CHUNK - core + 1) // 2
    hi = position // 2

    def excess_of(s, rs):
        excess = functools.reduce(jnp.maximum, split(s)) - best[rs, :]
        return jnp.max(excess.reshape(BLOCK // 8, 8, HEAD), axis=0)

    def flag_of(over):
        return (jnp.max(over) > SLACK).astype(jnp.int32)

    def first_scores():
        key = (2 * lo + core) * CHUNK + lax.broadcasted_iota(jnp.int32, (1, CHUNK), 1)
        seen = key >= first_start
        over = None
        for r in range(0, rows, BLOCK):
            rs = slice(r, r + BLOCK)
            s = jnp.where(seen, scores(q[rs, :], kv[lo, 0]), LOWEST)
            here[rs, :] = s
            excess = excess_of(s, rs)
            over = excess if over is None else jnp.maximum(over, excess)
        return flag_of(over)

    def mend(now):
        def block(i, carry):
            rs = pl.ds(pl.multiple_of(i * BLOCK, BLOCK), BLOCK)
            old = best[rs, :]
            new = jnp.maximum(old, jnp.max(now[rs, :], axis=1, keepdims=True))
            shrink = jnp.exp2((old - new) * LOG2_SCALE)
            best[rs, :] = new
            total[rs, :] = total[rs, :] * shrink
            acc[rs, :] = acc[rs, :] * shrink
            return carry

        lax.fori_loop(0, rows // BLOCK, block, 0)

    def step(tile, now, later, stale):
        @pl.when(stale > 0)
        def _():
            mend(now)

        ahead = jnp.minimum(tile + 1, hi - 1)
        over = None
        for r in range(0, rows, BLOCK):
            rs = slice(r, r + BLOCK)
            s = scores(q[rs, :], kv[ahead, 0])
            later[rs, :] = s
            excess = excess_of(s, rs)
            over = excess if over is None else jnp.maximum(over, excess)
            base = best[rs, :] * LOG2_SCALE
            weights = [jnp.exp2(part * LOG2_SCALE - base) for part in split(now[rs, :])]
            total[rs, :] += sum(weights)
            low = jnp.concatenate([w.astype(jnp.bfloat16) for w in weights], 1)
            acc[rs, :] += jnp.dot(low, kv[tile, 1], preferred_element_type=jnp.float32)
        return flag_of(over)

    def fast(tile, count):
        lane = lax.broadcasted_iota(jnp.int32, (1, CHUNK), 1)
        keys = [(2 * (tile + i) + core) * CHUNK + lane for i in range(count)]
        seen = [(key >= first_start) & (key < hi * 2 * CHUNK) for key in keys]

        def score(r):
            return [
                jnp.where(seen[i], scores(q[r : r + BLOCK, :], kv[tile + i, 0]), LOWEST)
                for i in range(count)
            ]

        def add(r, low):
            acc[r : r + BLOCK, :] += sum(
                jnp.dot(part, kv[tile + i, 1], preferred_element_type=jnp.float32)
                for i, part in enumerate(low)
            )

        s = score(0)
        waiting = None
        for r in range(0, rows, BLOCK):
            later = score(r + BLOCK) if r + BLOCK < rows else None
            if waiting is not None:
                add(*waiting)
            rs = slice(r, r + BLOCK)
            base = best[rs, :] * LOG2_SCALE
            weights = [
                [jnp.exp2(part * LOG2_SCALE - base) for part in split(block)] for block in s
            ]
            total[rs, :] += sum(w for row in weights for w in row)
            low = [jnp.concatenate([w.astype(jnp.bfloat16) for w in row], 1) for row in weights]
            waiting, s = (r, low), later
        add(*waiting)

    @pl.when(lo < hi)
    def _():
        peak = jnp.zeros((8, HEAD), jnp.float32)
        for i in range(kv.shape[0]):
            size = jnp.abs(kv[i, 0].astype(jnp.float32))
            peak = jnp.maximum(peak, jnp.max(size.reshape(CHUNK // 8, 8, HEAD), axis=0))
        peak = jnp.max(peak, axis=0, keepdims=True)
        size = jnp.sum(jnp.square(peak), axis=1, keepdims=True)
        bound = jnp.sqrt(size * reach[0, :1]) * 1.01 - reach[1, :1]
        near = jnp.max(bound) < REACH

        @pl.when(near)
        def _():
            count = hi - lo

            def pair(i, carry):
                fast(lo + 2 * i, 2)
                return carry

            lax.fori_loop(0, count // 2, pair, 0)

            @pl.when(lax.rem(count, 2) == 1)
            def _():
                fast(hi - 1, 1)

        @pl.when(jnp.logical_not(near))
        def _():
            stale = first_scores()

            def pair(i, stale):
                tile = lo + 2 * i
                stale = step(tile, here, there, stale)
                return lax.cond(
                    tile + 1 < hi,
                    lambda flag: step(tile + 1, there, here, flag),
                    lambda flag: flag,
                    stale,
                )

            lax.fori_loop(0, (hi - lo + 1) // 2, pair, stale)


def middle_kernel(lengths, q, kv, reach, near_best, best, total, acc, here, there):
    best[...] = near_best[...]
    total[...] = jnp.zeros(total.shape, jnp.float32)
    acc[...] = jnp.zeros(acc.shape, jnp.float32)
    fold_chunks(lengths, q, kv, reach, best, total, acc, here, there, True)


def last_kernel(
    lengths,
    q,
    kv,
    near_best,
    near_total,
    near_acc,
    reach,
    best_in,
    total_in,
    acc_in,
    out,
    best,
    total,
    acc,
    here,
    there,
):
    for r in range(0, out.shape[0], BLOCK):
        rs = slice(r, r + BLOCK)
        shrink = jnp.exp2((near_best[rs, :] - best_in[rs, :]) * LOG2_SCALE)
        best[rs, :] = best_in[rs, :]
        total[rs, :] = total_in[rs, :] + near_total[rs, :] * shrink
        acc[rs, :] = acc_in[rs, :] + near_acc[rs, :] * shrink
    fold_chunks(lengths, q, kv, reach, best, total, acc, here, there, False)
    for r in range(0, out.shape[0], BLOCK):
        rs = slice(r, r + BLOCK)
        out[rs, :] = (acc[rs, :] / jnp.sum(total[rs, :], axis=1, keepdims=True)).astype(out.dtype)


def per_device(queries, keys, values, doc_lengths):
    tokens, heads, _ = queries.shape
    rows = tokens * heads
    q = queries.reshape(rows, HEAD)
    spread = jnp.broadcast_to(
        jnp.stack([keys[:, 0], values[:, 0]])[None], (8, 2, tokens, HEAD)
    )
    near_keys, near_values = lax.optimization_barrier((keys, values))
    kv = jnp.stack([near_keys[:, 0], near_values[:, 0]])
    groups = [[2 * i + core for i in range(8)] for core in range(2)]
    swap = [(i, i ^ 1) for i in range(16)]
    mine = lax.all_to_all(spread, "ctx", 0, 0, axis_index_groups=groups)
    partner = lax.ppermute(kv, "ctx", swap)

    smem = pl.BlockSpec(memory_space=pltpu.SMEM)
    vmem = pl.BlockSpec(memory_space=pltpu.VMEM)
    params = pltpu.CompilerParams(vmem_limit_bytes=VMEM_LIMIT)
    wide = jax.ShapeDtypeStruct((rows, HEAD), jnp.float32)
    holds = [pltpu.VMEM((rows, CHUNK), jnp.float32)] * 2
    near = pl.pallas_call(
        local_kernel,
        out_shape=(wide, wide, wide, jax.ShapeDtypeStruct((2, 8, HEAD), jnp.float32)),
        in_specs=[smem, vmem, vmem, vmem],
        out_specs=(vmem, vmem, vmem, vmem),
        scratch_shapes=[pltpu.VMEM((rows, HEAD), jnp.int32)],
        compiler_params=params,
        cost_estimate=pl.CostEstimate(
            flops=6 * rows * CHUNK * HEAD * 4, bytes_accessed=2**24, transcendentals=0
        ),
    )(doc_lengths, q, kv, partner)
    mine, near_best = lax.optimization_barrier((mine, near[0]))
    theirs = lax.ppermute(mine, "ctx", swap)
    far = pl.pallas_call(
        middle_kernel,
        out_shape=(wide, wide, wide),
        in_specs=[smem] + [vmem] * 4,
        out_specs=(vmem, vmem, vmem),
        scratch_shapes=holds,
        compiler_params=params,
        cost_estimate=pl.CostEstimate(
            flops=14 * rows * CHUNK * HEAD * 4, bytes_accessed=2**24, transcendentals=0
        ),
    )(doc_lengths, q, mine, near[3], near_best)
    out = pl.pallas_call(
        last_kernel,
        out_shape=jax.ShapeDtypeStruct((rows, HEAD), jnp.bfloat16),
        in_specs=[smem] + [vmem] * 9,
        out_specs=vmem,
        scratch_shapes=[pltpu.VMEM((rows, HEAD), jnp.float32)] * 3 + holds,
        compiler_params=params,
        cost_estimate=pl.CostEstimate(
            flops=14 * rows * CHUNK * HEAD * 4, bytes_accessed=2**24, transcendentals=0
        ),
    )(doc_lengths, q, theirs, *near, *far)
    return out.reshape(queries.shape)


def solution(mesh):
    placed = (
        P(("dp", "ctx"), "tp", None),
        P(("dp", "ctx"), "tp", None),
        P(("dp", "ctx"), "tp", None),
        P("dp"),
    )
    return jax.shard_map(
        per_device,
        mesh=mesh,
        in_specs=placed,
        out_specs=P(("dp", "ctx"), "tp", None),
        check_vma=False,
    )
```

```python
import functools

import jax
import jax.numpy as jnp
from jax import lax
from jax.experimental import pallas as pl
from jax.experimental.pallas import tpu as pltpu
from jax.sharding import PartitionSpec as P

HEAD = 128
CHUNK = 256
BLOCK = 512
PART = 256
LOG2_SCALE = HEAD**-0.5 * 1.4426950408889634
LOWEST = -1e30
HIDDEN = 1e30
SLACK = 40.0 / LOG2_SCALE
REACH = 100.0 / LOG2_SCALE
VMEM_LIMIT = 20 * 2**20


def place(lengths):
    position = lax.axis_index("ctx")
    first = position * CHUNK
    begin = jnp.int32(0)
    first_start = jnp.int32(0)
    begins = []
    for doc in range(lengths.shape[0]):
        begins.append(begin)
        first_start = jnp.where(first >= begin, begin, first_start)
        begin = begin + lengths[doc]
    return position, first, first_start, begins


def scores(q, key):
    return lax.dot_general(q, key, (((1,), (1,)), ((), ())), preferred_element_type=jnp.float32)


def split(block):
    return [block[:, j : j + HEAD] for j in range(0, CHUNK, HEAD)]


def hide(block, chunk, first, row0, group, starts):
    done = []
    for j, part in enumerate(split(block)):
        key = chunk * CHUNK + j * HEAD + lax.broadcasted_iota(jnp.int32, part.shape, 1)
        row = first + (row0 + lax.broadcasted_iota(jnp.int32, part.shape, 0)) // group
        done.append(jnp.where((key >= starts) & (key <= row), part, LOWEST))
    return jnp.concatenate(done, 1)


def local_kernel(lengths, q, own, partner, best, total, acc, reach, starts):
    rows = q.shape[0]
    group = rows // CHUNK
    position, first, first_start, begins = place(lengths)
    core = lax.rem(position, 2)
    token = first + lax.broadcasted_iota(jnp.int32, (CHUNK, HEAD), 0)
    token_start = jnp.zeros((CHUNK, HEAD), jnp.int32)
    for begin in begins:
        token_start = jnp.where(token >= begin, begin, token_start)
    for head in range(group):
        starts[pl.ds(head, CHUNK, stride=group), :] = token_start
    best[...] = jnp.full(best.shape, LOWEST, jnp.float32)
    total[...] = jnp.zeros(total.shape, jnp.float32)
    acc[...] = jnp.zeros(acc.shape, jnp.float32)

    def fold(ref, chunk):
        def block(i, carry):
            rs = pl.ds(pl.multiple_of(i * BLOCK, BLOCK), BLOCK)
            s = hide(scores(q[rs, :], ref[0]), chunk, first, i * BLOCK, group, starts[rs, :])
            old = best[rs, :]
            new = jnp.maximum(old, jnp.max(s, axis=1, keepdims=True))
            shrink = jnp.exp2((old - new) * LOG2_SCALE)
            base = new * LOG2_SCALE
            weights = [jnp.exp2(part * LOG2_SCALE - base) for part in split(s)]
            best[rs, :] = new
            total[rs, :] = total[rs, :] * shrink + sum(weights)
            low = jnp.concatenate([w.astype(jnp.bfloat16) for w in weights], 1)
            acc[rs, :] = acc[rs, :] * shrink + jnp.dot(
                low, ref[1], preferred_element_type=jnp.float32
            )
            return carry

        lax.fori_loop(0, rows // BLOCK, block, 0)

    @pl.when(core == 1)
    def _():
        fold(partner, position - 1)

    fold(own, position)
    longest = jnp.zeros((8, HEAD), jnp.float32)
    least = jnp.full((8, HEAD), HIDDEN, jnp.float32)
    for r in range(0, rows, BLOCK):
        rs = slice(r, r + BLOCK)
        kept = jnp.where(starts[rs, :] == first_start, best[rs, :], HIDDEN)
        best[rs, :] = kept
        least = jnp.minimum(least, jnp.min(kept.reshape(BLOCK // 8, 8, HEAD), axis=0))
        squares = jnp.square(q[rs, :].astype(jnp.float32))
        norms = jnp.broadcast_to(jnp.sum(squares, axis=1, keepdims=True), squares.shape)
        longest = jnp.maximum(longest, jnp.max(norms.reshape(BLOCK // 8, 8, HEAD), axis=0))
    reach[0] = jnp.broadcast_to(jnp.max(longest, axis=0, keepdims=True), (8, HEAD))
    reach[1] = jnp.broadcast_to(jnp.min(least, axis=0, keepdims=True), (8, HEAD))


def bounded(kv, reach):
    peak = jnp.zeros((8, HEAD), jnp.float32)
    for i in range(kv.shape[0]):
        size = jnp.abs(kv[i, 0].astype(jnp.float32))
        peak = jnp.maximum(peak, jnp.max(size.reshape(CHUNK // 8, 8, HEAD), axis=0))
    peak = jnp.max(peak, axis=0, keepdims=True)
    size = jnp.sum(jnp.square(peak), axis=1, keepdims=True)
    return jnp.max(jnp.sqrt(size * reach[0, :1]) * 1.01 - reach[1, :1]) < REACH


def fold_chunks(lengths, q, kv, near, best, total, acc, here, there, mine):
    rows = q.shape[0]
    position, _, first_start, _ = place(lengths)
    core = lax.rem(position, 2)
    core = core if mine else 1 - core
    lo = (first_start // CHUNK - core + 1) // 2
    hi = position // 2

    def excess_of(s, rs):
        excess = functools.reduce(jnp.maximum, split(s)) - best[rs, :]
        return jnp.max(excess.reshape(BLOCK // 8, 8, HEAD), axis=0)

    def flag_of(over):
        return (jnp.max(over) > SLACK).astype(jnp.int32)

    def first_scores():
        key = (2 * lo + core) * CHUNK + lax.broadcasted_iota(jnp.int32, (1, CHUNK), 1)
        seen = key >= first_start
        over = None
        for r in range(0, rows, BLOCK):
            rs = slice(r, r + BLOCK)
            s = jnp.where(seen, scores(q[rs, :], kv[lo, 0]), LOWEST)
            here[rs, :] = s
            excess = excess_of(s, rs)
            over = excess if over is None else jnp.maximum(over, excess)
        return flag_of(over)

    def mend(now):
        def block(i, carry):
            rs = pl.ds(pl.multiple_of(i * BLOCK, BLOCK), BLOCK)
            old = best[rs, :]
            new = jnp.maximum(old, jnp.max(now[rs, :], axis=1, keepdims=True))
            shrink = jnp.exp2((old - new) * LOG2_SCALE)
            best[rs, :] = new
            total[rs, :] = total[rs, :] * shrink
            acc[rs, :] = acc[rs, :] * shrink
            return carry

        lax.fori_loop(0, rows // BLOCK, block, 0)

    def step(tile, now, later, stale):
        @pl.when(stale > 0)
        def _():
            mend(now)

        ahead = jnp.minimum(tile + 1, hi - 1)
        over = None
        for r in range(0, rows, BLOCK):
            rs = slice(r, r + BLOCK)
            s = scores(q[rs, :], kv[ahead, 0])
            later[rs, :] = s
            excess = excess_of(s, rs)
            over = excess if over is None else jnp.maximum(over, excess)
            base = best[rs, :] * LOG2_SCALE
            weights = [jnp.exp2(part * LOG2_SCALE - base) for part in split(now[rs, :])]
            total[rs, :] += sum(weights)
            low = jnp.concatenate([w.astype(jnp.bfloat16) for w in weights], 1)
            acc[rs, :] += jnp.dot(low, kv[tile, 1], preferred_element_type=jnp.float32)
        return flag_of(over)

    def fast(tile, count):
        lane = lax.broadcasted_iota(jnp.int32, (1, CHUNK), 1)
        keys = [(2 * (tile + i) + core) * CHUNK + lane for i in range(count)]
        seen = [(key >= first_start) & (key < hi * 2 * CHUNK) for key in keys]

        def score(r):
            return [
                jnp.where(seen[i], scores(q[r : r + PART, :], kv[tile + i, 0]), LOWEST)
                for i in range(count)
            ]

        def add(r, low):
            acc[r : r + PART, :] += sum(
                jnp.dot(part, kv[tile + i, 1], preferred_element_type=jnp.float32)
                for i, part in enumerate(low)
            )

        s = score(0)
        waiting = None
        for r in range(0, rows, PART):
            later = score(r + PART) if r + PART < rows else None
            if waiting is not None:
                add(*waiting)
            rs = slice(r, r + PART)
            base = best[rs, :] * LOG2_SCALE
            weights = [
                [jnp.exp2(part * LOG2_SCALE - base) for part in split(block)] for block in s
            ]
            total[rs, :] += sum(w for row in weights for w in row)
            low = [jnp.concatenate([w.astype(jnp.bfloat16) for w in row], 1) for row in weights]
            waiting, s = (r, low), later
        add(*waiting)

    @pl.when(lo < hi)
    def _():
        @pl.when(near)
        def _():
            count = hi - lo

            def pair(i, carry):
                fast(lo + 2 * i, 2)
                return carry

            lax.fori_loop(0, count // 2, pair, 0)

            @pl.when(lax.rem(count, 2) == 1)
            def _():
                fast(hi - 1, 1)

        @pl.when(jnp.logical_not(near))
        def _():
            stale = first_scores()

            def pair(i, stale):
                tile = lo + 2 * i
                stale = step(tile, here, there, stale)
                return lax.cond(
                    tile + 1 < hi,
                    lambda flag: step(tile + 1, there, here, flag),
                    lambda flag: flag,
                    stale,
                )

            lax.fori_loop(0, (hi - lo + 1) // 2, pair, stale)


def middle_kernel(lengths, q, kv, reach, near_best, best, total, acc, here, there):
    near = bounded(kv, reach)
    best[...] = near_best[...]
    total[...] = jnp.zeros(total.shape, jnp.float32)
    acc[...] = jnp.zeros(acc.shape, jnp.float32)
    fold_chunks(lengths, q, kv, near, best, total, acc, here, there, True)


def last_kernel(
    lengths,
    q,
    kv,
    near_best,
    near_total,
    near_acc,
    reach,
    best_in,
    total_in,
    acc_in,
    out,
    best,
    total,
    acc,
    here,
    there,
):
    near = bounded(kv, reach)
    for r in range(0, out.shape[0], BLOCK):
        rs = slice(r, r + BLOCK)
        shrink = jnp.exp2((near_best[rs, :] - best_in[rs, :]) * LOG2_SCALE)
        best[rs, :] = best_in[rs, :]
        total[rs, :] = total_in[rs, :] + near_total[rs, :] * shrink
        acc[rs, :] = acc_in[rs, :] + near_acc[rs, :] * shrink
    fold_chunks(lengths, q, kv, near, best, total, acc, here, there, False)
    for r in range(0, out.shape[0], BLOCK):
        rs = slice(r, r + BLOCK)
        out[rs, :] = (acc[rs, :] / jnp.sum(total[rs, :], axis=1, keepdims=True)).astype(out.dtype)


def per_device(queries, keys, values, doc_lengths):
    tokens, heads, _ = queries.shape
    rows = tokens * heads
    q = queries.reshape(rows, HEAD)
    spread = jnp.broadcast_to(
        jnp.stack([keys[:, 0], values[:, 0]])[None], (8, 2, tokens, HEAD)
    )
    near_keys, near_values = lax.optimization_barrier((keys, values))
    kv = jnp.stack([near_keys[:, 0], near_values[:, 0]])
    groups = [[2 * i + core for i in range(8)] for core in range(2)]
    swap = [(i, i ^ 1) for i in range(16)]
    mine = lax.all_to_all(spread, "ctx", 0, 0, axis_index_groups=groups)
    partner = lax.ppermute(kv, "ctx", swap)

    smem = pl.BlockSpec(memory_space=pltpu.SMEM)
    vmem = pl.BlockSpec(memory_space=pltpu.VMEM)
    params = pltpu.CompilerParams(vmem_limit_bytes=VMEM_LIMIT)
    wide = jax.ShapeDtypeStruct((rows, HEAD), jnp.float32)
    holds = [pltpu.VMEM((rows, CHUNK), jnp.float32)] * 2
    near = pl.pallas_call(
        local_kernel,
        out_shape=(wide, wide, wide, jax.ShapeDtypeStruct((2, 8, HEAD), jnp.float32)),
        in_specs=[smem, vmem, vmem, vmem],
        out_specs=(vmem, vmem, vmem, vmem),
        scratch_shapes=[pltpu.VMEM((rows, HEAD), jnp.int32)],
        compiler_params=params,
        cost_estimate=pl.CostEstimate(
            flops=6 * rows * CHUNK * HEAD * 4, bytes_accessed=2**24, transcendentals=0
        ),
    )(doc_lengths, q, kv, partner)
    mine, near_best = lax.optimization_barrier((mine, near[0]))
    theirs = lax.ppermute(mine, "ctx", swap)
    far = pl.pallas_call(
        middle_kernel,
        out_shape=(wide, wide, wide),
        in_specs=[smem] + [vmem] * 4,
        out_specs=(vmem, vmem, vmem),
        scratch_shapes=holds,
        compiler_params=params,
        cost_estimate=pl.CostEstimate(
            flops=14 * rows * CHUNK * HEAD * 4, bytes_accessed=2**24, transcendentals=0
        ),
    )(doc_lengths, q, mine, near[3], near_best)
    out = pl.pallas_call(
        last_kernel,
        out_shape=jax.ShapeDtypeStruct((rows, HEAD), jnp.bfloat16),
        in_specs=[smem] + [vmem] * 9,
        out_specs=vmem,
        scratch_shapes=[pltpu.VMEM((rows, HEAD), jnp.float32)] * 3 + holds,
        compiler_params=params,
        cost_estimate=pl.CostEstimate(
            flops=14 * rows * CHUNK * HEAD * 4, bytes_accessed=2**24, transcendentals=0
        ),
    )(doc_lengths, q, theirs, *near, *far)
    return out.reshape(queries.shape)


def solution(mesh):
    placed = (
        P(("dp", "ctx"), "tp", None),
        P(("dp", "ctx"), "tp", None),
        P(("dp", "ctx"), "tp", None),
        P("dp"),
    )
    return jax.shard_map(
        per_device,
        mesh=mesh,
        in_specs=placed,
        out_specs=P(("dp", "ctx"), "tp", None),
        check_vma=False,
    )
```

```python
import functools

import jax
import jax.numpy as jnp
from jax import lax
from jax.experimental import pallas as pl
from jax.experimental.pallas import tpu as pltpu
from jax.sharding import PartitionSpec as P

HEAD = 128
CHUNK = 256
BLOCK = 512
PART = 256
LOG2_SCALE = HEAD**-0.5 * 1.4426950408889634
LOWEST = -1e30
HIDDEN = 1e30
SLACK = 40.0 / LOG2_SCALE
REACH = 100.0 / LOG2_SCALE
VMEM_LIMIT = 20 * 2**20


def place(lengths):
    position = lax.axis_index("ctx")
    first = position * CHUNK
    begin = jnp.int32(0)
    first_start = jnp.int32(0)
    begins = []
    for doc in range(lengths.shape[0]):
        begins.append(begin)
        first_start = jnp.where(first >= begin, begin, first_start)
        begin = begin + lengths[doc]
    return position, first, first_start, begins


def scores(q, key):
    return lax.dot_general(q, key, (((1,), (1,)), ((), ())), preferred_element_type=jnp.float32)


def split(block):
    return [block[:, j : j + HEAD] for j in range(0, CHUNK, HEAD)]


def hide(block, chunk, first, row0, group, starts):
    done = []
    for j, part in enumerate(split(block)):
        key = chunk * CHUNK + j * HEAD + lax.broadcasted_iota(jnp.int32, part.shape, 1)
        row = first + (row0 + lax.broadcasted_iota(jnp.int32, part.shape, 0)) // group
        done.append(jnp.where((key >= starts) & (key <= row), part, LOWEST))
    return jnp.concatenate(done, 1)


def local_kernel(lengths, q, own, partner, best, total, acc, reach, starts):
    rows = q.shape[0]
    group = rows // CHUNK
    position, first, first_start, begins = place(lengths)
    core = lax.rem(position, 2)
    token = first + lax.broadcasted_iota(jnp.int32, (CHUNK, HEAD), 0)
    token_start = jnp.zeros((CHUNK, HEAD), jnp.int32)
    for begin in begins:
        token_start = jnp.where(token >= begin, begin, token_start)
    for head in range(group):
        starts[pl.ds(head, CHUNK, stride=group), :] = token_start
    best[...] = jnp.full(best.shape, LOWEST, jnp.float32)
    total[...] = jnp.zeros(total.shape, jnp.float32)
    acc[...] = jnp.zeros(acc.shape, jnp.float32)

    def fold(ref, chunk):
        def block(i, carry):
            rs = pl.ds(pl.multiple_of(i * BLOCK, BLOCK), BLOCK)
            s = hide(scores(q[rs, :], ref[0]), chunk, first, i * BLOCK, group, starts[rs, :])
            old = best[rs, :]
            new = jnp.maximum(old, jnp.max(s, axis=1, keepdims=True))
            shrink = jnp.exp2((old - new) * LOG2_SCALE)
            base = new * LOG2_SCALE
            weights = [jnp.exp2(part * LOG2_SCALE - base) for part in split(s)]
            best[rs, :] = new
            total[rs, :] = total[rs, :] * shrink + sum(weights)
            low = jnp.concatenate([w.astype(jnp.bfloat16) for w in weights], 1)
            acc[rs, :] = acc[rs, :] * shrink + jnp.dot(
                low, ref[1], preferred_element_type=jnp.float32
            )
            return carry

        lax.fori_loop(0, rows // BLOCK, block, 0)

    @pl.when(core == 1)
    def _():
        fold(partner, position - 1)

    fold(own, position)
    longest = jnp.zeros((8, HEAD), jnp.float32)
    least = jnp.full((8, HEAD), HIDDEN, jnp.float32)
    for r in range(0, rows, BLOCK):
        rs = slice(r, r + BLOCK)
        kept = jnp.where(starts[rs, :] == first_start, best[rs, :], HIDDEN)
        best[rs, :] = kept
        least = jnp.minimum(least, jnp.min(kept.reshape(BLOCK // 8, 8, HEAD), axis=0))
        squares = jnp.square(q[rs, :].astype(jnp.float32))
        norms = jnp.broadcast_to(jnp.sum(squares, axis=1, keepdims=True), squares.shape)
        longest = jnp.maximum(longest, jnp.max(norms.reshape(BLOCK // 8, 8, HEAD), axis=0))
    reach[0] = jnp.broadcast_to(jnp.max(longest, axis=0, keepdims=True), (8, HEAD))
    reach[1] = jnp.broadcast_to(jnp.min(least, axis=0, keepdims=True), (8, HEAD))


def bounded(kv, reach):
    peak = jnp.zeros((8, HEAD), jnp.float32)
    for i in range(kv.shape[0]):
        size = jnp.abs(kv[i, 0].astype(jnp.float32))
        peak = jnp.maximum(peak, jnp.max(size.reshape(CHUNK // 8, 8, HEAD), axis=0))
    peak = jnp.max(peak, axis=0, keepdims=True)
    size = jnp.sum(jnp.square(peak), axis=1, keepdims=True)
    return jnp.max(jnp.sqrt(size * reach[0, :1]) * 1.01 - reach[1, :1]) < REACH


def fold_chunks(lengths, q, kv, near, level, best, total, acc, here, there, mine):
    rows = q.shape[0]
    position, _, first_start, _ = place(lengths)
    core = lax.rem(position, 2)
    core = core if mine else 1 - core
    lo = (first_start // CHUNK - core + 1) // 2
    hi = position // 2

    def excess_of(s, rs):
        excess = functools.reduce(jnp.maximum, split(s)) - best[rs, :]
        return jnp.max(excess.reshape(BLOCK // 8, 8, HEAD), axis=0)

    def flag_of(over):
        return (jnp.max(over) > SLACK).astype(jnp.int32)

    def first_scores():
        key = (2 * lo + core) * CHUNK + lax.broadcasted_iota(jnp.int32, (1, CHUNK), 1)
        seen = key >= first_start
        over = None
        for r in range(0, rows, BLOCK):
            rs = slice(r, r + BLOCK)
            s = jnp.where(seen, scores(q[rs, :], kv[lo, 0]), LOWEST)
            here[rs, :] = s
            excess = excess_of(s, rs)
            over = excess if over is None else jnp.maximum(over, excess)
        return flag_of(over)

    def mend(now):
        def block(i, carry):
            rs = pl.ds(pl.multiple_of(i * BLOCK, BLOCK), BLOCK)
            old = best[rs, :]
            new = jnp.maximum(old, jnp.max(now[rs, :], axis=1, keepdims=True))
            shrink = jnp.exp2((old - new) * LOG2_SCALE)
            best[rs, :] = new
            total[rs, :] = total[rs, :] * shrink
            acc[rs, :] = acc[rs, :] * shrink
            return carry

        lax.fori_loop(0, rows // BLOCK, block, 0)

    def step(tile, now, later, stale):
        @pl.when(stale > 0)
        def _():
            mend(now)

        ahead = jnp.minimum(tile + 1, hi - 1)
        over = None
        for r in range(0, rows, BLOCK):
            rs = slice(r, r + BLOCK)
            s = scores(q[rs, :], kv[ahead, 0])
            later[rs, :] = s
            excess = excess_of(s, rs)
            over = excess if over is None else jnp.maximum(over, excess)
            base = best[rs, :] * LOG2_SCALE
            weights = [jnp.exp2(part * LOG2_SCALE - base) for part in split(now[rs, :])]
            total[rs, :] += sum(weights)
            low = jnp.concatenate([w.astype(jnp.bfloat16) for w in weights], 1)
            acc[rs, :] += jnp.dot(low, kv[tile, 1], preferred_element_type=jnp.float32)
        return flag_of(over)

    def fast(tile, count):
        lane = lax.broadcasted_iota(jnp.int32, (1, CHUNK), 1)
        keys = [(2 * (tile + i) + core) * CHUNK + lane for i in range(count)]
        seen = [(key >= first_start) & (key < hi * 2 * CHUNK) for key in keys]

        def score(r):
            return [
                jnp.where(seen[i], scores(q[r : r + PART, :], kv[tile + i, 0]), LOWEST)
                for i in range(count)
            ]

        def add(r, low):
            acc[r : r + PART, :] += sum(
                jnp.dot(part, kv[tile + i, 1], preferred_element_type=jnp.float32)
                for i, part in enumerate(low)
            )

        s = score(0)
        waiting = None
        for r in range(0, rows, PART):
            later = score(r + PART) if r + PART < rows else None
            if waiting is not None:
                add(*waiting)
            rs = slice(r, r + PART)
            base = level[rs, :] * LOG2_SCALE
            weights = [
                [jnp.exp2(part * LOG2_SCALE - base) for part in split(block)] for block in s
            ]
            total[rs, :] += sum(w for row in weights for w in row)
            low = [jnp.concatenate([w.astype(jnp.bfloat16) for w in row], 1) for row in weights]
            waiting, s = (r, low), later
        add(*waiting)

    @pl.when(lo < hi)
    def _():
        @pl.when(near)
        def _():
            count = hi - lo

            def pair(i, carry):
                fast(lo + 2 * i, 2)
                return carry

            lax.fori_loop(0, count // 2, pair, 0)

            @pl.when(lax.rem(count, 2) == 1)
            def _():
                fast(hi - 1, 1)

        @pl.when(jnp.logical_not(near))
        def _():
            best[...] = level[...]
            stale = first_scores()

            def pair(i, stale):
                tile = lo + 2 * i
                stale = step(tile, here, there, stale)
                return lax.cond(
                    tile + 1 < hi,
                    lambda flag: step(tile + 1, there, here, flag),
                    lambda flag: flag,
                    stale,
                )

            lax.fori_loop(0, (hi - lo + 1) // 2, pair, stale)


def middle_kernel(lengths, q, kv, reach, near_best, best, total, acc, here, there):
    near = bounded(kv, reach)
    best[...] = near_best[...]
    total[...] = jnp.zeros(total.shape, jnp.float32)
    acc[...] = jnp.zeros(acc.shape, jnp.float32)
    fold_chunks(lengths, q, kv, near, near_best, best, total, acc, here, there, True)


def last_kernel(
    lengths,
    q,
    kv,
    near_best,
    near_total,
    near_acc,
    reach,
    best_in,
    total_in,
    acc_in,
    out,
    best,
    total,
    acc,
    here,
    there,
    ready,
    sems,
):
    near = bounded(kv, reach)
    for r in range(0, out.shape[0], BLOCK):
        rs = slice(r, r + BLOCK)
        shrink = jnp.exp2((near_best[rs, :] - best_in[rs, :]) * LOG2_SCALE)
        total[rs, :] = total_in[rs, :] + near_total[rs, :] * shrink
        acc[rs, :] = acc_in[rs, :] + near_acc[rs, :] * shrink
    fold_chunks(lengths, q, kv, near, best_in, best, total, acc, here, there, False)
    copies = []
    for i, r in enumerate(range(0, out.shape[0], BLOCK)):
        rs = slice(r, r + BLOCK)
        mixed = acc[rs, :] / jnp.sum(total[rs, :], axis=1, keepdims=True)
        ready[rs, :] = mixed.astype(out.dtype)
        copies.append(
            pltpu.make_async_copy(
                ready.at[pl.ds(r, BLOCK), :], out.at[pl.ds(r, BLOCK), :], sems.at[i]
            )
        )
        copies[-1].start()
    for copy in copies:
        copy.wait()


def per_device(queries, keys, values, doc_lengths):
    tokens, heads, _ = queries.shape
    rows = tokens * heads
    q = queries.reshape(rows, HEAD)
    spread = jnp.broadcast_to(
        jnp.stack([keys[:, 0], values[:, 0]])[None], (8, 2, tokens, HEAD)
    )
    near_keys, near_values = lax.optimization_barrier((keys, values))
    kv = jnp.stack([near_keys[:, 0], near_values[:, 0]])
    groups = [[2 * i + core for i in range(8)] for core in range(2)]
    swap = [(i, i ^ 1) for i in range(16)]
    mine = lax.all_to_all(spread, "ctx", 0, 0, axis_index_groups=groups)
    partner = lax.ppermute(kv, "ctx", swap)

    smem = pl.BlockSpec(memory_space=pltpu.SMEM)
    vmem = pl.BlockSpec(memory_space=pltpu.VMEM)
    params = pltpu.CompilerParams(vmem_limit_bytes=VMEM_LIMIT)
    wide = jax.ShapeDtypeStruct((rows, HEAD), jnp.float32)
    holds = [pltpu.VMEM((rows, CHUNK), jnp.float32)] * 2
    near = pl.pallas_call(
        local_kernel,
        out_shape=(wide, wide, wide, jax.ShapeDtypeStruct((2, 8, HEAD), jnp.float32)),
        in_specs=[smem, vmem, vmem, vmem],
        out_specs=(vmem, vmem, vmem, vmem),
        scratch_shapes=[pltpu.VMEM((rows, HEAD), jnp.int32)],
        compiler_params=params,
        cost_estimate=pl.CostEstimate(
            flops=6 * rows * CHUNK * HEAD * 4, bytes_accessed=2**24, transcendentals=0
        ),
    )(doc_lengths, q, kv, partner)
    mine, near_best = lax.optimization_barrier((mine, near[0]))
    theirs = lax.ppermute(mine, "ctx", swap)
    far = pl.pallas_call(
        middle_kernel,
        out_shape=(wide, wide, wide),
        in_specs=[smem] + [vmem] * 4,
        out_specs=(vmem, vmem, vmem),
        scratch_shapes=holds,
        compiler_params=params,
        cost_estimate=pl.CostEstimate(
            flops=14 * rows * CHUNK * HEAD * 4, bytes_accessed=2**24, transcendentals=0
        ),
    )(doc_lengths, q, mine, near[3], near_best)
    out = pl.pallas_call(
        last_kernel,
        out_shape=jax.ShapeDtypeStruct((rows, HEAD), jnp.bfloat16),
        in_specs=[smem] + [vmem] * 9,
        out_specs=pl.BlockSpec(memory_space=pl.ANY),
        scratch_shapes=[pltpu.VMEM((rows, HEAD), jnp.float32)] * 3
        + holds
        + [pltpu.VMEM((rows, HEAD), jnp.bfloat16), pltpu.SemaphoreType.DMA((rows // BLOCK,))],
        compiler_params=params,
        cost_estimate=pl.CostEstimate(
            flops=14 * rows * CHUNK * HEAD * 4, bytes_accessed=2**24, transcendentals=0
        ),
    )(doc_lengths, q, theirs, *near, *far)
    return out.reshape(queries.shape)


def solution(mesh):
    placed = (
        P(("dp", "ctx"), "tp", None),
        P(("dp", "ctx"), "tp", None),
        P(("dp", "ctx"), "tp", None),
        P("dp"),
    )
    return jax.shard_map(
        per_device,
        mesh=mesh,
        in_specs=placed,
        out_specs=P(("dp", "ctx"), "tp", None),
        check_vma=False,
    )
```
